768 devices in a mesh: gx: 8 (over y), gy: 8 (over x, core), gz: 12 (over z).
Axes of the slice: x: 4, y: 8, z: 12, core: 2. Of those that a mesh axis runs over, the one named last changes fastest.
Arguments:
- tensor_field: bfloat16 [64, 24, 512, 512], P(None, 'gz', 'gx', 'gy'), may hold values from -80 to 80
- start_x: float32 [512, 256], replicated, may hold values from -5 to 5
- start_y: float32 [512, 256], replicated, may hold values from -5 to 5
Outputs:
- basis_x: float32 [512, 256], P('gx')
- basis_y: float32 [512, 256], P('gy')
- core_tensor: bfloat16 [64, 24, 256, 256], P('gx', 'gz', 'gy')
The draws below stay inside these ranges and needn't reach their ends.
All inputs are finite; a program needn't handle non-finite values.
Results may differ from the reference program's by a relative error of at most 0.009.
Values may be sent and summed in bfloat16 or wider, within the bound.
A program may use at most 64 MiB of HBM per device.

```python
import jax
import jax.numpy as jnp
from jax import lax

NX = 512
NY = 512
S = 64
R1 = 256
R2 = 256
ITERS = 3
NZ = 24


def draw_tensor_field(key, part):
    key = jax.random.fold_in(key, 11)
    subkeys = jax.random.split(key, 4)
    noise = jax.random.truncated_normal(subkeys[0], -4.0, 4.0, (S, NZ, NX, NY), jnp.float32)
    upper = 2.0
    scale_x = jnp.exp(jax.random.uniform(subkeys[1], (NX,), jnp.float32, 0.0, 1.0) * jnp.log(upper))
    scale_y = jnp.exp(jax.random.uniform(subkeys[2], (NY,), jnp.float32, 0.0, 1.0) * jnp.log(upper))
    positions_x = jnp.arange(NX, dtype=jnp.float32)
    positions_y = jnp.arange(NY, dtype=jnp.float32)
    signal = jnp.zeros((S, NZ, NX, NY), jnp.float32)
    for wave_index in range(4):
        wave_keys = jax.random.split(jax.random.fold_in(subkeys[3], wave_index), 5)
        freq_x = 0.03 + 1.57 * jnp.power(jax.random.uniform(wave_keys[0], (S, NZ), jnp.float32, 0.0, 1.0), 1.5)
        freq_y = 0.03 + 1.57 * jnp.power(jax.random.uniform(wave_keys[1], (S, NZ), jnp.float32, 0.0, 1.0), 1.5)
        phase_x = jax.random.uniform(wave_keys[2], (S, NZ), jnp.float32, -3.14159, 3.14159)
        phase_y = jax.random.uniform(wave_keys[3], (S, NZ), jnp.float32, -3.14159, 3.14159)
        amplitude = jax.random.uniform(wave_keys[4], (S, NZ), jnp.float32, -1.732, 1.732)
        wave_x = jnp.cos(freq_x[:, :, None] * positions_x[None, None, :] + phase_x[:, :, None])
        wave_y = jnp.cos(freq_y[:, :, None] * positions_y[None, None, :] + phase_y[:, :, None])
        signal = signal + amplitude[:, :, None, None] * wave_x[:, :, :, None] * wave_y[:, :, None, :]
    values = scale_x[None, None, :, None] * scale_y[None, None, None, :] * (noise + signal)
    return values.astype(jnp.bfloat16)


def bell_draw(rng, dims, deviation, most, held_as=jnp.bfloat16):
    array = deviation * jax.random.normal(rng, dims, jnp.float32)
    return jnp.clip(array, min=-most, max=most).astype(held_as)


def setup_inputs(seed: int = 0) -> dict:
    key_of = jax.random.split(jax.random.key(seed), 4)
    return {
        "tensor_field": draw_tensor_field(jax.random.fold_in(key_of[3], 71), 0),
        "start_x": bell_draw(key_of[1], (NX, R1), 1.0, 5.0, jnp.float32),
        "start_y": bell_draw(key_of[2], (NY, R2), 1.0, 5.0, jnp.float32),
    }


def subspace(gram_matrix, start):
    current = start
    for sweep in range(ITERS):
        product = jnp.dot(gram_matrix, current, precision=lax.Precision.HIGHEST)
        inner_gram = jnp.dot(product.T, product, precision=lax.Precision.HIGHEST)
        lower_factor = jnp.linalg.cholesky(inner_gram)
        current = jax.scipy.linalg.solve_triangular(lower_factor, product.T, lower=True).T
    return current

def reference(tensor_field, start_x, start_y):

    def add_x(total, species_block):
        flattened = jnp.transpose(species_block, (1, 0, 2)).reshape(NX, -1)
        return (total + jnp.dot(flattened.astype(jnp.float32), flattened.T.astype(jnp.float32), preferred_element_type=jnp.float32), None)
    gram_x, unused = lax.scan(add_x, jnp.zeros((NX, NX), jnp.float32), tensor_field)
    gram_x = gram_x * (1.0 / (S * NZ * NY))
    basis_x = subspace(gram_x, start_x)
    low_x = basis_x.astype(jnp.bfloat16)

    def project_x(species_block):
        return jnp.einsum('xr,zxy->zry', low_x.astype(jnp.float32), species_block.astype(jnp.float32)).astype(jnp.bfloat16)
    partial_core = lax.map(project_x, tensor_field)

    def add_y(total, species_block):
        flattened = species_block.reshape(-1, NY)
        return (total + jnp.dot(flattened.T.astype(jnp.float32), flattened.astype(jnp.float32), preferred_element_type=jnp.float32), None)
    gram_y, unused = lax.scan(add_y, jnp.zeros((NY, NY), jnp.float32), partial_core)
    gram_y = gram_y * (1.0 / (S * NZ * R1))
    basis_y = subspace(gram_y, start_y)
    low_y = basis_y.astype(jnp.bfloat16)

    def project_y(species_block):
        return jnp.einsum('zry,yq->zrq', species_block.astype(jnp.float32), low_y.astype(jnp.float32)).astype(jnp.bfloat16)
    core_tensor = lax.map(project_y, partial_core)
    return (basis_x, basis_y, core_tensor)
```

```python
import functools

import jax
import jax.numpy as jnp
from jax import lax
from jax.experimental import pallas as pl
from jax.experimental.pallas import tpu as pltpu
from jax.sharding import PartitionSpec as P

ITERS = 3
PANEL = 32
TILE = 128
EXACT = lax.Precision.HIGHEST
MESH = pl.DeviceIdType.MESH
f32 = jnp.float32
bf16 = jnp.bfloat16


def split3(value):
    high = value.astype(bf16)
    rest = value - high.astype(f32)
    middle = rest.astype(bf16)
    low = (rest - middle.astype(f32)).astype(bf16)
    return high, middle, low


def row_of(value, index):
    return jnp.broadcast_to(value[index : index + 1, :], (8, TILE))


def column_of(value, index):
    return jnp.broadcast_to(value[:, index : index + 1], (8, TILE))


def factor(work):
    n = work.shape[0]
    sub = lax.broadcasted_iota(jnp.int32, (8, TILE), 0)
    groups = PANEL // 8
    for top in range(0, n, PANEL):
        below = top + PANEL
        first = (top // TILE) * TILE
        last = -(-below // TILE) * TILE
        lanes = list(range(first, n, TILE)) + list(range(n, n + last, TILE))
        panel = [
            [work[top + 8 * g : top + 8 * g + 8, at : at + TILE] for g in range(groups)]
            for at in lanes
        ]
        for g in range(groups):
            offset = top + 8 * g - first
            spread = [
                [column_of(panel[0][s], offset + k) if s >= g else None for s in range(groups)]
                for k in range(8)
            ]
            pivots = jnp.ones((8, TILE), f32)
            for j in range(8):
                pivot = row_of(spread[j][g], j)
                pivots = jnp.where(sub == j, pivot, pivots)
                inverse = 1.0 / pivot
                rows = [row_of(column[g], j) for column in panel]
                heads = [row_of(spread[k][g], j) for k in range(j + 1, 8)]
                for s in range(g, groups):
                    times = spread[j][s] * inverse
                    if s == g:
                        if j == 7:
                            continue
                        times = jnp.where(sub > j, times, 0.0)
                    for a, row in enumerate(rows):
                        panel[a][s] = panel[a][s] - times * row
                    for k in range(j + 1, 8):
                        spread[k][s] = spread[k][s] - times * heads[k - j - 1]
            scale = lax.rsqrt(pivots)
            for column in panel:
                column[g] = column[g] * scale
        done = [jnp.concatenate(column, 0) for column in panel]
        for at, block in zip(lanes, done):
            if at >= n:
                work[top:below, at : at + TILE] = block
        if below < n:
            high, middle, low = split3(jnp.concatenate(done, 1))
            right = jnp.concatenate([high, middle, low, high, middle, high], 0)
            left = jnp.concatenate([high, high, high, middle, middle, low], 0)[:, : n - first]
            update = lax.dot_general(left, right, (((0,), (0,)), ((), ())), preferred_element_type=f32)
            update = update[below - first :, :]
            for a, at in enumerate(lanes):
                work[below:, at : at + TILE] -= update[:, TILE * a : TILE * (a + 1)]


def unpack(packed_ref, gram_ref, scale):
    blocks = gram_ref.shape[0] // TILE
    at = 0
    for i in range(blocks):
        for c in range(i + 1):
            block = packed_ref[at : at + TILE, :] * scale
            gram_ref[i * TILE : (i + 1) * TILE, c * TILE : (c + 1) * TILE] = block
            if c < i:
                gram_ref[c * TILE : (c + 1) * TILE, i * TILE : (i + 1) * TILE] = block.T
            at += TILE


def subspace(gram_ref, start, work):
    rank = work.shape[0]
    row = lax.broadcasted_iota(jnp.int32, (rank, rank), 0)
    column = lax.broadcasted_iota(jnp.int32, (rank, rank), 1)
    current = start
    for sweep in range(ITERS):
        product = jnp.dot(gram_ref[...], current, precision=EXACT, preferred_element_type=f32)
        work[:, :rank] = lax.dot_general(
            product, product, (((0,), (0,)), ((), ())), precision=EXACT, preferred_element_type=f32
        )
        work[:, rank:] = jnp.where(row == column, 1.0, 0.0)
        factor(work)
        current = lax.dot_general(
            product, work[:, rank:], (((1,), (1,)), ((), ())), precision=EXACT, preferred_element_type=f32
        )
    return current


def basis_x_kernel(scale, packed_ref, start_ref, own_ref, low_ref, gram, work, basis):
    unpack(packed_ref, gram, scale)
    basis[...] = subspace(gram, start_ref[...], work)
    low_ref[...] = basis[...].astype(bf16)
    rows = own_ref.shape[0]
    own_ref[...] = basis[pl.ds(pl.multiple_of(lax.axis_index("gx") * rows, rows), rows), :]


def basis_y_kernel(scale, packed_ref, start_ref, field_ref, own_ref, core_ref, gram, work, basis):
    unpack(packed_ref, gram, scale)
    basis[...] = subspace(gram, start_ref[...], work)
    core_ref[...] = jnp.dot(
        field_ref[...], basis[...].astype(bf16), preferred_element_type=f32
    ).astype(bf16)
    rows = own_ref.shape[0]
    own_ref[...] = basis[pl.ds(pl.multiple_of(lax.axis_index("gy") * rows, rows), rows), :]


def send(source, target, send_sem, recv_sem, axis, device):
    copy = pltpu.make_async_remote_copy(
        src_ref=source,
        dst_ref=target,
        send_sem=send_sem,
        recv_sem=recv_sem,
        device_id={axis: device},
        device_id_type=MESH,
    )
    copy.start()
    return copy


def greet(sizes):
    barrier = pltpu.get_barrier_semaphore()
    for axis, size in sizes.items():
        me = lax.axis_index(axis)
        for d in range(1, size):
            pl.semaphore_signal(
                barrier, inc=1, device_id={axis: lax.rem(me + d, size)}, device_id_type=MESH
            )


def await_greetings(sizes):
    pl.semaphore_wait(pltpu.get_barrier_semaphore(), sum(size - 1 for size in sizes.values()))


def share_of(rows, size):
    tiles = rows // 8
    length = -(-tiles // size)
    return length * 8, lambda i: (i * tiles // size) * 8


def total(partial, result, sizes, s1, s2, s3, s4, mine, sems):
    nx, ny, nz = sizes["gx"], sizes["gy"], sizes["gz"]
    gx, gy, gz = lax.axis_index("gx"), lax.axis_index("gy"), lax.axis_index("gz")
    part = partial.shape[0] // ny
    share, begin = share_of(part, nx)
    out1, in1, out2, in2, out3, in3, out4, in4, out5, in5 = sems

    copies = []
    for d in range(1, ny):
        to = lax.rem(gy + d, ny)
        rows = pl.ds(pl.multiple_of(to * part, 8), part)
        copies.append(send(partial.at[rows], s1.at[d - 1], out1.at[d], in1.at[d], "gy", to))
    own = partial[pl.ds(pl.multiple_of(gy * part, 8), part), :]
    for d, copy in enumerate(copies):
        copy.wait_recv()
        own = own + s1[d]
    mine[...] = own
    waits = list(copies)

    copies = []
    for d in range(1, nx):
        to = lax.rem(gx + d, nx)
        rows = pl.ds(pl.multiple_of(begin(to), 8), share)
        copies.append(send(mine.at[rows], s2.at[d - 1], out2.at[d], in2.at[d], "gx", to))
    own = mine[pl.ds(pl.multiple_of(begin(gx), 8), share), :]
    for d, copy in enumerate(copies):
        copy.wait_recv()
        own = own + s2[d]
    waits += copies

    s3[gz] = own
    copies = []
    for d in range(1, nz):
        to = lax.rem(gz + d, nz)
        copies.append(send(s3.at[gz], s3.at[gz], out3.at[d], in3.at[d], "gz", to))
    for copy in copies:
        copy.wait_recv()
    waits += copies
    own = s3[0]
    for z in range(1, nz):
        own = own + s3[z]

    s4[gx] = own
    copies = []
    for d in range(1, nx):
        to = lax.rem(gx + d, nx)
        copies.append(send(s4.at[gx], s4.at[gx], out4.at[d], in4.at[d], "gx", to))
    for copy in copies:
        copy.wait_recv()
    waits += copies

    rows = pl.ds(pl.multiple_of(gy * part, 8), part)
    tiles = part // 8
    pieces = []
    for t in range(tiles):
        i = (t * nx) // tiles
        while i * tiles // nx + share // 8 <= t:
            i += 1
        while i * tiles // nx > t:
            i -= 1
        at = t * 8 - (i * tiles // nx) * 8
        pieces.append(s4[i, at : at + 8, :])
    result[rows, :] = jnp.concatenate(pieces, 0)
    copies = []
    for d in range(1, ny):
        to = lax.rem(gy + d, ny)
        copies.append(send(result.at[rows], result.at[rows], out5.at[d], in5.at[d], "gy", to))
    for copy in copies:
        copy.wait_recv()
    waits += copies
    for copy in waits:
        copy.wait_send()


def gram_x_kernel(sizes, field_ref, fibres_ref, gram_ref, outgoing, fibres, partial, result, s1, s2, s3, s4, mine, out0, in0, *sems):
    nx = sizes["gx"]
    gx = lax.axis_index("gx")
    species, planes, rows, width = field_ref.shape
    block = species // nx
    step = planes * width
    greet(sizes)

    def pack(to, put):
        for k in range(block):
            planes_of = [field_ref[to * block + k, z] for z in range(planes)]
            put(k, jnp.concatenate(planes_of, 1))

    own_rows = pl.ds(pl.multiple_of(gx * rows, rows), rows)
    order = sorted(range(1, nx), key=lambda d: -min(d, nx - d))
    copies = []
    for count, d in enumerate(order):
        to = lax.rem(gx + d, nx)

        def put(k, value, d=d):
            outgoing[d - 1, :, k * step : (k + 1) * step] = value

        pack(to, put)
        if count == 0:
            await_greetings(sizes)
        copies.append(send(outgoing.at[d - 1], fibres.at[own_rows], out0.at[d], in0.at[d], "gx", to))

    def put_own(k, value):
        fibres[own_rows, k * step : (k + 1) * step] = value

    pack(gx, put_own)
    for copy in copies:
        copy.wait_recv()
    at = 0
    for i in range(fibres.shape[0] // TILE):
        found = lax.dot_general(
            fibres[i * TILE : (i + 1) * TILE, :],
            fibres[: (i + 1) * TILE, :],
            (((1,), (1,)), ((), ())),
            preferred_element_type=f32,
        )
        for c in range(i + 1):
            partial[at : at + TILE, :] = found[:, c * TILE : (c + 1) * TILE]
            at += TILE
    total(partial, result, sizes, s1, s2, s3, s4, mine, sems)
    fibres_ref[...] = fibres[...]
    gram_ref[...] = result[...]
    for copy in copies:
        copy.wait_send()


def gram_y_kernel(sizes, groups, low_ref, fibres_ref, matrix_ref, gram_ref, outgoing, blocks, matrix, partial, result, s1, s2, s3, s4, mine, out0, in0, *sems):
    ny = sizes["gy"]
    gy = lax.axis_index("gy")
    rank = low_ref.shape[1]
    part = rank // ny
    width = fibres_ref.shape[1] // groups
    greet(sizes)
    outgoing[...] = lax.dot_general(
        low_ref[...], fibres_ref[...], (((0,), (0,)), ((), ())), preferred_element_type=f32
    ).astype(bf16)
    await_greetings(sizes)
    copies = []
    for d in range(1, ny):
        to = lax.rem(gy + d, ny)
        rows = pl.ds(pl.multiple_of(to * part, part), part)
        copies.append(send(outgoing.at[rows], blocks.at[gy], out0.at[d], in0.at[d], "gy", to))
    blocks[gy] = outgoing[pl.ds(pl.multiple_of(gy * part, part), part), :]
    for copy in copies:
        copy.wait_recv()
    joined = TILE // width
    for m in range(ny // joined):
        for g in range(groups):
            pieces = [blocks[m * joined + h, :, g * width : (g + 1) * width] for h in range(joined)]
            matrix[g * part : (g + 1) * part, m * TILE : (m + 1) * TILE] = jnp.concatenate(pieces, 1)
    at = 0
    for i in range(matrix.shape[1] // TILE):
        found = lax.dot_general(
            matrix[:, i * TILE : (i + 1) * TILE],
            matrix[:, : (i + 1) * TILE],
            (((0,), (0,)), ((), ())),
            preferred_element_type=f32,
        )
        for c in range(i + 1):
            partial[at : at + TILE, :] = found[:, c * TILE : (c + 1) * TILE]
            at += TILE
    total(partial, result, sizes, s1, s2, s3, s4, mine, sems)
    matrix_ref[...] = matrix[...]
    gram_ref[...] = result[...]
    for copy in copies:
        copy.wait_send()


def total_scratch(n, sizes):
    blocks = n // TILE
    rows = blocks * (blocks + 1) // 2 * TILE
    nx, ny, nz = sizes["gx"], sizes["gy"], sizes["gz"]
    part = rows // ny
    share = share_of(part, nx)[0]
    buffers = [
        pltpu.VMEM((rows, TILE), f32),
        pltpu.VMEM((rows, TILE), f32),
        pltpu.VMEM((ny - 1, part, TILE), f32),
        pltpu.VMEM((nx - 1, share, TILE), f32),
        pltpu.VMEM((nz, share, TILE), f32),
        pltpu.VMEM((nx, share, TILE), f32),
        pltpu.VMEM((part, TILE), f32),
    ]
    sems = []
    for size in (ny, nx, nz, nx, ny):
        sems += [pltpu.SemaphoreType.DMA((size,)), pltpu.SemaphoreType.DMA((size,))]
    return rows, buffers, sems


def body(sizes, tensor_field, start_x, start_y):
    species, planes, rows_x, rows_y = tensor_field.shape
    nx, ny, nz = sizes["gx"], sizes["gy"], sizes["gz"]
    all_x, rank_x = start_x.shape
    all_y, rank_y = start_y.shape
    block = species // nx
    groups = block * planes
    width = groups * rows_y
    part = rank_x // ny
    vmem = pl.BlockSpec(memory_space=pltpu.VMEM)

    def communicating(kernel, outs, own, n, size, collective):
        rows, buffers, sems = total_scratch(n, sizes)
        exchange = [pltpu.SemaphoreType.DMA((size,)), pltpu.SemaphoreType.DMA((size,))]
        return pl.pallas_call(
            kernel,
            out_shape=outs + (jax.ShapeDtypeStruct((rows, TILE), f32),),
            in_specs=[vmem] * (1 if collective == 0 else 2),
            out_specs=(vmem,) * (len(outs) + 1),
            scratch_shapes=own + buffers + exchange + sems,
            compiler_params=pltpu.CompilerParams(
                collective_id=collective, has_side_effects=True, vmem_limit_bytes=48 << 20
            ),
        )

    fibres, packed_x = communicating(
        functools.partial(gram_x_kernel, sizes),
        (jax.ShapeDtypeStruct((all_x, width), bf16),),
        [pltpu.VMEM((nx - 1, rows_x, width), bf16), pltpu.VMEM((all_x, width), bf16)],
        all_x,
        nx,
        0,
    )(tensor_field)

    def scratch(n, rank):
        return [
            pltpu.VMEM((n, n), f32),
            pltpu.VMEM((rank, 2 * rank), f32),
            pltpu.VMEM((n, rank), f32),
        ]

    own_x, low_x = pl.pallas_call(
        functools.partial(basis_x_kernel, 1.0 / (species * planes * nz * all_y)),
        out_shape=(
            jax.ShapeDtypeStruct((all_x // nx, rank_x), f32),
            jax.ShapeDtypeStruct((all_x, rank_x), bf16),
        ),
        in_specs=[vmem] * 2,
        out_specs=(vmem,) * 2,
        scratch_shapes=scratch(all_x, rank_x),
        compiler_params=pltpu.CompilerParams(vmem_limit_bytes=48 << 20),
    )(packed_x, start_x)

    matrix, packed_y = communicating(
        functools.partial(gram_y_kernel, sizes, groups),
        (jax.ShapeDtypeStruct((groups * part, all_y), bf16),),
        [
            pltpu.VMEM((rank_x, width), bf16),
            pltpu.VMEM((ny, part, width), bf16),
            pltpu.VMEM((groups * part, all_y), bf16),
        ],
        all_y,
        ny,
        1,
    )(low_x, fibres)

    own_y, core = pl.pallas_call(
        functools.partial(basis_y_kernel, 1.0 / (species * planes * nz * rank_x)),
        out_shape=(
            jax.ShapeDtypeStruct((all_y // ny, rank_y), f32),
            jax.ShapeDtypeStruct((groups * part, rank_y), bf16),
        ),
        in_specs=[vmem] * 3,
        out_specs=(vmem,) * 2,
        scratch_shapes=scratch(all_y, rank_y),
        compiler_params=pltpu.CompilerParams(vmem_limit_bytes=48 << 20),
    )(packed_y, start_y, matrix)
    return own_x, own_y, core.reshape(block, planes, part, rank_y)


def solution(mesh):
    sizes = {axis: mesh.shape[axis] for axis in ("gx", "gy", "gz")}
    in_specs = (P(None, "gz", "gx", "gy"), P(), P())
    out_specs = (P("gx", None), P("gy", None), P("gx", "gz", "gy", None))
    return jax.shard_map(
        functools.partial(body, sizes), mesh=mesh, in_specs=in_specs, out_specs=out_specs, check_vma=False
    )
```

```python
import functools

import jax
import jax.numpy as jnp
from jax import lax
from jax.experimental import pallas as pl
from jax.experimental.pallas import tpu as pltpu
from jax.sharding import PartitionSpec as P

ITERS = 3
PANEL = 32
SPREAD = 16
TILE = 128
MESH = pl.DeviceIdType.MESH
f32 = jnp.float32
bf16 = jnp.bfloat16


def split3(value):
    high = value.astype(bf16)
    rest = value - high.astype(f32)
    middle = rest.astype(bf16)
    low = (rest - middle.astype(f32)).astype(bf16)
    return high, middle, low


def row_of(value, index):
    return jnp.broadcast_to(value[index : index + 1, :], (8, TILE))


def column_of(value, index):
    return jnp.broadcast_to(value[:, index : index + 1], (8, TILE))


def factor(work):
    n = work.shape[0]
    sub = lax.broadcasted_iota(jnp.int32, (8, TILE), 0)
    groups = PANEL // 8
    for top in range(0, n, PANEL):
        below = top + PANEL
        first = (top // TILE) * TILE
        last = -(-below // TILE) * TILE
        lanes = list(range(first, n, TILE)) + list(range(n, n + last, TILE))
        panel = [
            [work[top + 8 * g : top + 8 * g + 8, at : at + TILE] for g in range(groups)]
            for at in lanes
        ]
        for start in range(0, PANEL, SPREAD):
            offset = top + start - first
            spread = [
                [column_of(panel[0][s], offset + k) if 8 * s >= start else None for s in range(groups)]
                for k in range(SPREAD)
            ]
            for j in range(SPREAD):
                g, i = divmod(start + j, 8)
                if i == 0:
                    scales = jnp.ones((8, TILE), f32)
                scale = lax.rsqrt(row_of(spread[j][g], i))
                scales = jnp.where(sub == i, scale, scales)
                rows = [row_of(column[g], i) * scale for column in panel]
                heads = [row_of(spread[k][g], i) * scale for k in range(j + 1, SPREAD)]
                for s in range(g, groups):
                    times = spread[j][s] * scale
                    if s == g:
                        if i == 7:
                            continue
                        times = jnp.where(sub > i, times, 0.0)
                    for a, row in enumerate(rows):
                        panel[a][s] = panel[a][s] - times * row
                    for k, head in enumerate(heads, j + 1):
                        spread[k][s] = spread[k][s] - times * head
                if i == 7:
                    for column in panel:
                        column[g] = column[g] * scales
        done = [jnp.concatenate(column, 0) for column in panel]
        for at, block in zip(lanes, done):
            if at >= n:
                work[top:below, at : at + TILE] = block
        if below < n:
            high, middle, low = split3(jnp.concatenate(done, 1))
            right = jnp.concatenate([high, middle, low, high, middle, high], 0)
            left = jnp.concatenate([high, high, high, middle, middle, low], 0)[:, : n - first]
            update = lax.dot_general(left, right, (((0,), (0,)), ((), ())), preferred_element_type=f32)
            update = update[below - first :, :]
            for a, at in enumerate(lanes):
                work[below:, at : at + TILE] -= update[:, TILE * a : TILE * (a + 1)]


def unpack(packed_ref, gram_ref, scale):
    blocks = gram_ref.shape[0] // TILE
    at = 0
    for i in range(blocks):
        for c in range(i + 1):
            block = packed_ref[at : at + TILE, :] * scale
            gram_ref[i * TILE : (i + 1) * TILE, c * TILE : (c + 1) * TILE] = block
            if c < i:
                gram_ref[c * TILE : (c + 1) * TILE, i * TILE : (i + 1) * TILE] = block.T
            at += TILE


def dot(left, right, left_axis, right_axis):
    return lax.dot_general(left, right, (((left_axis,), (right_axis,)), ((), ())), preferred_element_type=f32)


def dot3(left, right, left_axis, right_axis):
    (a, b, _), (c, d, _) = left, right
    return (dot(b, c, left_axis, right_axis) + dot(a, d, left_axis, right_axis)) + dot(a, c, left_axis, right_axis)


def dot6(left, right, left_axis, right_axis):
    (a, b, c), (d, e, f) = left, right
    tail = (dot(c, d, left_axis, right_axis) + dot(b, e, left_axis, right_axis)) + dot(a, f, left_axis, right_axis)
    return tail + dot3(left, right, left_axis, right_axis)


def subspace(gram_ref, start, work):
    rank = work.shape[0]
    row = lax.broadcasted_iota(jnp.int32, (rank, rank), 0)
    column = lax.broadcasted_iota(jnp.int32, (rank, rank), 1)
    gram = split3(gram_ref[...])
    current = start
    for sweep in range(ITERS):
        product = split3(dot3(gram, split3(current), 1, 0))
        work[:, :rank] = dot6(product, product, 0, 0)
        work[:, rank:] = jnp.where(row == column, 1.0, 0.0)
        factor(work)
        current = dot3(product, split3(work[:, rank:]), 1, 1)
    return current


def basis_x_kernel(scale, packed_ref, start_ref, own_ref, low_ref, gram, work, basis):
    unpack(packed_ref, gram, scale)
    basis[...] = subspace(gram, start_ref[...], work)
    low_ref[...] = basis[...].astype(bf16)
    rows = own_ref.shape[0]
    own_ref[...] = basis[pl.ds(pl.multiple_of(lax.axis_index("gx") * rows, rows), rows), :]


def basis_y_kernel(scale, packed_ref, start_ref, field_ref, own_ref, core_ref, gram, work, basis):
    unpack(packed_ref, gram, scale)
    basis[...] = subspace(gram, start_ref[...], work)
    core_ref[...] = jnp.dot(
        field_ref[...], basis[...].astype(bf16), preferred_element_type=f32
    ).astype(bf16)
    rows = own_ref.shape[0]
    own_ref[...] = basis[pl.ds(pl.multiple_of(lax.axis_index("gy") * rows, rows), rows), :]


def send(source, target, send_sem, recv_sem, axis, device):
    copy = pltpu.make_async_remote_copy(
        src_ref=source,
        dst_ref=target,
        send_sem=send_sem,
        recv_sem=recv_sem,
        device_id={axis: device},
        device_id_type=MESH,
    )
    copy.start()
    return copy


def greet(sizes):
    barrier = pltpu.get_barrier_semaphore()
    for axis, size in sizes.items():
        me = lax.axis_index(axis)
        for d in range(1, size):
            pl.semaphore_signal(
                barrier, inc=1, device_id={axis: lax.rem(me + d, size)}, device_id_type=MESH
            )


def await_greetings(sizes):
    pl.semaphore_wait(pltpu.get_barrier_semaphore(), sum(size - 1 for size in sizes.values()))


def share_of(rows, size):
    tiles = rows // 8
    length = -(-tiles // size)
    return length * 8, lambda i: (i * tiles // size) * 8


def nearest(size):
    return sorted(range(size), key=lambda d: min(d, size - d))


def total(partial, result, sizes, pair, s1, s2, s3, s4, mine, sems):
    nx, ny, nz = sizes["gx"], sizes["gy"], sizes["gz"]
    gx, gy, gz = lax.axis_index("gx"), lax.axis_index("gy"), lax.axis_index("gz")
    chips = ny // 2
    core = lax.rem(gy, 2)
    chip = gy // 2
    partner = gy + 1 - 2 * core
    part = partial.shape[0] // ny
    share, begin = share_of(part, nx)
    out0, in0, out1, in1, out2, in2, out3, in3, out4, in4, out5, in5, out6, in6 = sems
    waits = []

    def chunk(index):
        return pl.ds(pl.multiple_of(index * part, 8), part)

    far_first = nearest(chips)[::-1]
    given = {}
    for f in far_first:
        to = lax.rem(chip + f, chips) * 2 + 1 - core
        given[f] = send(partial.at[chunk(to)], pair.at[f], out0.at[f], in0.at[f], "gy", partner)
    scattered = []
    for f in far_first:
        to = lax.rem(chip + f, chips) * 2 + core
        given[f].wait_recv()
        mine[f] = partial[chunk(to), :] + pair[f]
        if f:
            scattered.append(send(mine.at[f], s1.at[f - 1], out1.at[f], in1.at[f], "gy", to))
    for copy in scattered:
        copy.wait_recv()
    own = mine[0]
    for f in range(chips - 1):
        own = own + s1[f]
    mine[0] = own
    waits += list(given.values()) + scattered

    copies = []
    for d in nearest(nx)[:0:-1]:
        to = lax.rem(gx + d, nx)
        rows = pl.ds(pl.multiple_of(begin(to), 8), share)
        copies.append(send(mine.at[0, rows], s2.at[d - 1], out2.at[d], in2.at[d], "gx", to))
    for copy in copies:
        copy.wait_recv()
    own = mine[0, pl.ds(pl.multiple_of(begin(gx), 8), share), :]
    for d in range(nx - 1):
        own = own + s2[d]
    waits += copies

    s3[gz] = own
    copies = []
    for d in nearest(nz)[:0:-1]:
        to = lax.rem(gz + d, nz)
        copies.append(send(s3.at[gz], s3.at[gz], out3.at[d], in3.at[d], "gz", to))
    for copy in copies:
        copy.wait_recv()
    waits += copies
    own = s3[0]
    for z in range(1, nz):
        own = own + s3[z]

    s4[gx] = own
    copies = []
    for d in nearest(nx)[:0:-1]:
        to = lax.rem(gx + d, nx)
        copies.append(send(s4.at[gx], s4.at[gx], out4.at[d], in4.at[d], "gx", to))
    for copy in copies:
        copy.wait_recv()
    waits += copies

    pieces = []
    for at in range(0, part, 8):
        x = max(x for x in range(nx) if begin(x) <= at)
        pieces.append(s4[x, at - begin(x) : at - begin(x) + 8, :])
    result[chunk(gy), :] = jnp.concatenate(pieces, 0)
    across = {}
    for f in far_first[:-1]:
        to = lax.rem(chip + f, chips) * 2 + core
        across[f] = send(result.at[chunk(gy)], result.at[chunk(gy)], out5.at[f], in5.at[f], "gy", to)
    copies = []
    for f in far_first[::-1]:
        source = lax.rem(chip + chips - f, chips) * 2 + core
        if f:
            across[f].wait_recv()
        copies.append(send(result.at[chunk(source)], result.at[chunk(source)], out6.at[f], in6.at[f], "gy", partner))
    for copy in copies:
        copy.wait_recv()
    waits += list(across.values()) + copies
    for copy in waits:
        copy.wait_send()


def gram_x_kernel(sizes, field_ref, fibres_ref, gram_ref, field, loaded, outgoing, fibres, partial, result, pair, s1, s2, s3, s4, mine, out0, in0, *sems):
    nx = sizes["gx"]
    gx = lax.axis_index("gx")
    species, planes, rows, width = field_ref.shape
    block = species // nx
    step = planes * width
    order = nearest(nx)[::-1]
    loads = {}
    for d in order:
        part = pl.ds(lax.rem(gx + d, nx) * block, block)
        loads[d] = pltpu.make_async_copy(field_ref.at[part], field.at[part], loaded.at[d])
        loads[d].start()
    greet(sizes)

    def pack(to, put):
        for k in range(block):
            planes_of = [field[to * block + k, z] for z in range(planes)]
            put(k, jnp.concatenate(planes_of, 1))

    own_rows = pl.ds(pl.multiple_of(gx * rows, rows), rows)
    copies = []
    for count, d in enumerate(order[:-1]):
        to = lax.rem(gx + d, nx)

        def put(k, value, d=d):
            outgoing[d - 1, :, k * step : (k + 1) * step] = value

        loads[d].wait()
        pack(to, put)
        if count == 0:
            await_greetings(sizes)
        copies.append(send(outgoing.at[d - 1], fibres.at[own_rows], out0.at[d], in0.at[d], "gx", to))

    def put_own(k, value):
        fibres[own_rows, k * step : (k + 1) * step] = value

    loads[0].wait()
    pack(gx, put_own)
    for copy in copies:
        copy.wait_recv()
    at = 0
    for i in range(fibres.shape[0] // TILE):
        found = lax.dot_general(
            fibres[i * TILE : (i + 1) * TILE, :],
            fibres[: (i + 1) * TILE, :],
            (((1,), (1,)), ((), ())),
            preferred_element_type=f32,
        )
        for c in range(i + 1):
            partial[at : at + TILE, :] = found[:, c * TILE : (c + 1) * TILE]
            at += TILE
    total(partial, result, sizes, pair, s1, s2, s3, s4, mine, sems)
    fibres_ref[...] = fibres[...]
    gram_ref[...] = result[...]
    for copy in copies:
        copy.wait_send()


def gram_y_kernel(sizes, groups, low_ref, fibres_ref, matrix_ref, gram_ref, outgoing, blocks, matrix, partial, result, pair, s1, s2, s3, s4, mine, out0, in0, *sems):
    ny = sizes["gy"]
    gy = lax.axis_index("gy")
    rank = low_ref.shape[1]
    part = rank // ny
    width = fibres_ref.shape[1] // groups
    greet(sizes)
    outgoing[...] = lax.dot_general(
        low_ref[...], fibres_ref[...], (((0,), (0,)), ((), ())), preferred_element_type=f32
    ).astype(bf16)
    await_greetings(sizes)
    copies = []
    for d in range(1, ny):
        to = lax.rem(gy + d, ny)
        rows = pl.ds(pl.multiple_of(to * part, part), part)
        copies.append(send(outgoing.at[rows], blocks.at[gy], out0.at[d], in0.at[d], "gy", to))
    blocks[gy] = outgoing[pl.ds(pl.multiple_of(gy * part, part), part), :]
    for copy in copies:
        copy.wait_recv()
    joined = TILE // width
    for m in range(ny // joined):
        for g in range(groups):
            pieces = [blocks[m * joined + h, :, g * width : (g + 1) * width] for h in range(joined)]
            matrix[g * part : (g + 1) * part, m * TILE : (m + 1) * TILE] = jnp.concatenate(pieces, 1)
    at = 0
    for i in range(matrix.shape[1] // TILE):
        found = lax.dot_general(
            matrix[:, i * TILE : (i + 1) * TILE],
            matrix[:, : (i + 1) * TILE],
            (((0,), (0,)), ((), ())),
            preferred_element_type=f32,
        )
        for c in range(i + 1):
            partial[at : at + TILE, :] = found[:, c * TILE : (c + 1) * TILE]
            at += TILE
    total(partial, result, sizes, pair, s1, s2, s3, s4, mine, sems)
    matrix_ref[...] = matrix[...]
    gram_ref[...] = result[...]
    for copy in copies:
        copy.wait_send()


def total_scratch(n, sizes):
    blocks = n // TILE
    rows = blocks * (blocks + 1) // 2 * TILE
    nx, ny, nz = sizes["gx"], sizes["gy"], sizes["gz"]
    part = rows // ny
    share = share_of(part, nx)[0]
    chips = ny // 2
    buffers = [
        pltpu.VMEM((rows, TILE), f32),
        pltpu.VMEM((rows, TILE), f32),
        pltpu.VMEM((chips, part, TILE), f32),
        pltpu.VMEM((chips - 1, part, TILE), f32),
        pltpu.VMEM((nx - 1, share, TILE), f32),
        pltpu.VMEM((nz, share, TILE), f32),
        pltpu.VMEM((nx, share, TILE), f32),
        pltpu.VMEM((chips, part, TILE), f32),
    ]
    sems = []
    for size in (chips, chips, nx, nz, nx, chips, chips):
        sems += [pltpu.SemaphoreType.DMA((size,)), pltpu.SemaphoreType.DMA((size,))]
    return rows, buffers, sems


def body(sizes, tensor_field, start_x, start_y):
    species, planes, rows_x, rows_y = tensor_field.shape
    nx, ny, nz = sizes["gx"], sizes["gy"], sizes["gz"]
    all_x, rank_x = start_x.shape
    all_y, rank_y = start_y.shape
    block = species // nx
    groups = block * planes
    width = groups * rows_y
    part = rank_x // ny
    vmem = pl.BlockSpec(memory_space=pltpu.VMEM)

    def communicating(kernel, outs, own, n, size, collective):
        rows, buffers, sems = total_scratch(n, sizes)
        exchange = [pltpu.SemaphoreType.DMA((size,)), pltpu.SemaphoreType.DMA((size,))]
        return pl.pallas_call(
            kernel,
            out_shape=outs + (jax.ShapeDtypeStruct((rows, TILE), f32),),
            in_specs=[pl.BlockSpec(memory_space=pl.ANY)] if collective == 0 else [vmem] * 2,
            out_specs=(vmem,) * (len(outs) + 1),
            scratch_shapes=own + buffers + exchange + sems,
            compiler_params=pltpu.CompilerParams(
                collective_id=collective, has_side_effects=True, vmem_limit_bytes=48 << 20
            ),
        )

    fibres, packed_x = communicating(
        functools.partial(gram_x_kernel, sizes),
        (jax.ShapeDtypeStruct((all_x, width), bf16),),
        [
            pltpu.VMEM(tensor_field.shape, bf16),
            pltpu.SemaphoreType.DMA((nx,)),
            pltpu.VMEM((nx - 1, rows_x, width), bf16),
            pltpu.VMEM((all_x, width), bf16),
        ],
        all_x,
        nx,
        0,
    )(tensor_field)

    def scratch(n, rank):
        return [
            pltpu.VMEM((n, n), f32),
            pltpu.VMEM((rank, 2 * rank), f32),
            pltpu.VMEM((n, rank), f32),
        ]

    own_x, low_x = pl.pallas_call(
        functools.partial(basis_x_kernel, 1.0 / (species * planes * nz * all_y)),
        out_shape=(
            jax.ShapeDtypeStruct((all_x // nx, rank_x), f32),
            jax.ShapeDtypeStruct((all_x, rank_x), bf16),
        ),
        in_specs=[vmem] * 2,
        out_specs=(vmem,) * 2,
        scratch_shapes=scratch(all_x, rank_x),
        compiler_params=pltpu.CompilerParams(vmem_limit_bytes=48 << 20),
    )(packed_x, start_x)

    matrix, packed_y = communicating(
        functools.partial(gram_y_kernel, sizes, groups),
        (jax.ShapeDtypeStruct((groups * part, all_y), bf16),),
        [
            pltpu.VMEM((rank_x, width), bf16),
            pltpu.VMEM((ny, part, width), bf16),
            pltpu.VMEM((groups * part, all_y), bf16),
        ],
        all_y,
        ny,
        1,
    )(low_x, fibres)

    own_y, core = pl.pallas_call(
        functools.partial(basis_y_kernel, 1.0 / (species * planes * nz * rank_x)),
        out_shape=(
            jax.ShapeDtypeStruct((all_y // ny, rank_y), f32),
            jax.ShapeDtypeStruct((groups * part, rank_y), bf16),
        ),
        in_specs=[vmem] * 3,
        out_specs=(vmem,) * 2,
        scratch_shapes=scratch(all_y, rank_y),
        compiler_params=pltpu.CompilerParams(vmem_limit_bytes=48 << 20),
    )(packed_y, start_y, matrix)
    return own_x, own_y, core.reshape(block, planes, part, rank_y)


def solution(mesh):
    sizes = {axis: mesh.shape[axis] for axis in ("gx", "gy", "gz")}
    in_specs = (P(None, "gz", "gx", "gy"), P(), P())
    out_specs = (P("gx", None), P("gy", None), P("gx", "gz", "gy", None))
    return jax.shard_map(
        functools.partial(body, sizes), mesh=mesh, in_specs=in_specs, out_specs=out_specs, check_vma=False
    )
```

```python
import functools

import jax
import jax.numpy as jnp
from jax import lax
from jax.experimental import pallas as pl
from jax.experimental.pallas import tpu as pltpu
from jax.sharding import PartitionSpec as P

ITERS = 3
PANEL = 32
SPREAD = 16
TILE = 128
CHUNK = TILE + 8
MESH = pl.DeviceIdType.MESH
f32 = jnp.float32
bf16 = jnp.bfloat16


def split3(value):
    high = value.astype(bf16)
    rest = value - high.astype(f32)
    middle = rest.astype(bf16)
    low = (rest - middle.astype(f32)).astype(bf16)
    return high, middle, low


def row_of(value, index):
    return jnp.broadcast_to(value[index : index + 1, :], (8, TILE))


def column_of(value, index):
    return jnp.broadcast_to(value[:, index : index + 1], (8, TILE))


def factor(work):
    n = work.shape[0]
    sub = lax.broadcasted_iota(jnp.int32, (8, TILE), 0)
    groups = PANEL // 8
    for top in range(0, n, PANEL):
        below = top + PANEL
        first = (top // TILE) * TILE
        last = -(-below // TILE) * TILE
        lanes = list(range(first, n, TILE)) + list(range(n, n + last, TILE))
        panel = [
            [work[top + 8 * g : top + 8 * g + 8, at : at + TILE] for g in range(groups)]
            for at in lanes
        ]
        for start in range(0, PANEL, SPREAD):
            offset = top + start - first
            spread = [
                [column_of(panel[0][s], offset + k) if 8 * s >= start else None for s in range(groups)]
                for k in range(SPREAD)
            ]
            for j in range(SPREAD):
                g, i = divmod(start + j, 8)
                if i == 0:
                    scales = jnp.ones((8, TILE), f32)
                scale = lax.rsqrt(row_of(spread[j][g], i))
                scales = jnp.where(sub == i, scale, scales)
                rows = [row_of(column[g], i) * scale for column in panel]
                heads = [row_of(spread[k][g], i) * scale for k in range(j + 1, SPREAD)]
                for s in range(g, groups):
                    times = spread[j][s] * scale
                    if s == g:
                        if i == 7:
                            continue
                        times = jnp.where(sub > i, times, 0.0)
                    for a, row in enumerate(rows):
                        panel[a][s] = panel[a][s] - times * row
                    for k, head in enumerate(heads, j + 1):
                        spread[k][s] = spread[k][s] - times * head
                if i == 7:
                    for column in panel:
                        column[g] = column[g] * scales
        done = [jnp.concatenate(column, 0) for column in panel]
        for at, block in zip(lanes, done):
            if at >= n:
                work[top:below, at : at + TILE] = block
        if below < n:
            high, middle, low = split3(jnp.concatenate(done, 1))
            right = jnp.concatenate([high, middle, low, high, middle, high], 0)
            left = jnp.concatenate([high, high, high, middle, middle, low], 0)[:, : n - first]
            update = lax.dot_general(left, right, (((0,), (0,)), ((), ())), preferred_element_type=f32)
            update = update[below - first :, :]
            for a, at in enumerate(lanes):
                work[below:, at : at + TILE] -= update[:, TILE * a : TILE * (a + 1)]


def masks(size):
    row = lax.broadcasted_iota(jnp.int32, (size, size), 0)
    column = lax.broadcasted_iota(jnp.int32, (size, size), 1)
    return row, column


def fold(partial, block):
    lower, first, second = block(1, 0), block(0, 0), block(1, 1)
    half = first.shape[0]
    row, column = masks(half)
    mixed = jnp.where(row > column, second, first)
    diagonal = jnp.sum(jnp.where(row == column, second, 0.0), axis=0, keepdims=True)
    sub = lax.broadcasted_iota(jnp.int32, (8, TILE), 0)
    at = 0
    for whole in (lower, mixed):
        for c in range(0, half, TILE):
            for r in range(0, half, TILE):
                partial[at : at + TILE, :] = whole[r : r + TILE, c : c + TILE]
                chunk = at // CHUNK
                if chunk * TILE < half:
                    piece = diagonal[:, chunk * TILE : (chunk + 1) * TILE]
                    extra = jnp.where(sub == 0, jnp.broadcast_to(piece, (8, TILE)), 0.0)
                else:
                    extra = jnp.zeros((8, TILE), f32)
                partial[at + TILE : at + CHUNK, :] = extra
                at += CHUNK


def unfold(packed_ref, gram_ref, scale):
    half = gram_ref.shape[0] // 2
    row, column = masks(half)
    side = half // TILE

    def whole(first):
        columns = []
        for c in range(side):
            starts = [(first + c * side + r) * CHUNK for r in range(side)]
            columns.append(jnp.concatenate([packed_ref[at : at + TILE, :] for at in starts], 0))
        return jnp.concatenate(columns, 1) * scale

    lower, mixed = whole(0), whole(side * side)
    ends = [packed_ref[k * CHUNK + TILE : k * CHUNK + TILE + 1, :] for k in range(side)]
    diagonal = jnp.broadcast_to(jnp.concatenate(ends, 1) * scale, (half, half))
    turned = mixed.T
    gram_ref[:half, :half] = jnp.where(row <= column, mixed, turned)
    gram_ref[:half, half:] = lower.T
    gram_ref[half:, :half] = lower
    gram_ref[half:, half:] = jnp.where(row > column, mixed, jnp.where(row == column, diagonal, turned))


def dot(left, right, left_axis, right_axis):
    return lax.dot_general(left, right, (((left_axis,), (right_axis,)), ((), ())), preferred_element_type=f32)


def dot3(left, right, left_axis, right_axis):
    (a, b, _), (c, d, _) = left, right
    return (dot(b, c, left_axis, right_axis) + dot(a, d, left_axis, right_axis)) + dot(a, c, left_axis, right_axis)


def inner(value):
    high, middle, low = value
    cross = dot(high, low, 1, 1) + dot(high, middle, 1, 1)
    return (dot(middle, middle, 1, 1) + (cross + cross.T)) + dot(high, high, 1, 1)


def subspace(gram_ref, start, work):
    rank = work.shape[0]
    row, column = masks(rank)
    gram = split3(gram_ref[...])
    for sweep in range(ITERS):
        if sweep == 0:
            product = split3(dot3(split3(start), gram, 0, 0))
        else:
            product = split3(dot3(split3(current), gram, 1, 0))
        work[:, :rank] = inner(product)
        work[:, rank:] = jnp.where(row == column, 1.0, 0.0)
        factor(work)
        current = dot3(split3(work[:, rank:]), product, 1, 0)
    return current


def own_rows(basis, axis, own_ref, block):
    rows = own_ref.shape[0]
    shares = TILE // rows
    me = lax.axis_index(axis)
    block[...] = basis[:, pl.ds(pl.multiple_of(me // shares * TILE, TILE), TILE)].T
    own_ref[...] = block[pl.ds(pl.multiple_of(lax.rem(me, shares) * rows, rows), rows), :]


def basis_x_kernel(scale, packed_ref, start_ref, own_ref, low_ref, gram, work, basis, block):
    unfold(packed_ref, gram, scale)
    basis[...] = subspace(gram, start_ref[...], work)
    low_ref[...] = basis[...].astype(bf16)
    own_rows(basis, "gx", own_ref, block)


def basis_y_kernel(scale, packed_ref, start_ref, field_ref, own_ref, core_ref, gram, work, basis, block):
    unfold(packed_ref, gram, scale)
    basis[...] = subspace(gram, start_ref[...], work)
    core_ref[...] = dot(field_ref[...], basis[...].astype(bf16), 1, 1).astype(bf16)
    own_rows(basis, "gy", own_ref, block)


def send(source, target, send_sem, recv_sem, axis, device):
    copy = pltpu.make_async_remote_copy(
        src_ref=source,
        dst_ref=target,
        send_sem=send_sem,
        recv_sem=recv_sem,
        device_id={axis: device},
        device_id_type=MESH,
    )
    copy.start()
    return copy


def greet(sizes):
    barrier = pltpu.get_barrier_semaphore()
    for axis, size in sizes.items():
        me = lax.axis_index(axis)
        for d in range(1, size):
            pl.semaphore_signal(
                barrier, inc=1, device_id={axis: lax.rem(me + d, size)}, device_id_type=MESH
            )


def await_greetings(sizes):
    pl.semaphore_wait(pltpu.get_barrier_semaphore(), sum(size - 1 for size in sizes.values()))


def nearest(size):
    return sorted(range(size), key=lambda d: min(d, size - d))


def total(partial, result, sizes, pair, s1, s2, s3, s4, mine, lines, sems):
    nx, ny, nz = sizes["gx"], sizes["gy"], sizes["gz"]
    gx, gy, gz = lax.axis_index("gx"), lax.axis_index("gy"), lax.axis_index("gz")
    chips = ny // 2
    core = lax.rem(gy, 2)
    chip = gy // 2
    partner = gy + 1 - 2 * core
    part = partial.shape[0] // ny
    share = part // nx
    out0, in0, out1, in1, out2, in2, out3, in3, out4, in4, out5, in5, out6, in6 = sems
    waits = []

    def chunk(index):
        return pl.ds(pl.multiple_of(index * part, 8), part)

    far_first = nearest(chips)[::-1]
    given = {}
    for f in far_first:
        to = lax.rem(chip + f, chips) * 2 + 1 - core
        given[f] = send(partial.at[chunk(to)], pair.at[f], out0.at[f], in0.at[f], "gy", partner)
    scattered = []
    for f in far_first:
        to = lax.rem(chip + f, chips) * 2 + core
        given[f].wait_recv()
        mine[f] = partial[chunk(to), :] + pair[f]
        if f:
            scattered.append(send(mine.at[f], s1.at[f - 1], out1.at[f], in1.at[f], "gy", to))
    for copy in scattered:
        copy.wait_recv()
    own = mine[0]
    for f in range(chips - 1):
        own = own + s1[f]
    lines[...] = own.reshape(lines.shape)
    waits += list(given.values()) + scattered

    copies = []
    for d in nearest(nx)[:0:-1]:
        to = lax.rem(gx + d, nx)
        copies.append(send(lines.at[pl.ds(to * share, share)], s2.at[d - 1], out2.at[d], in2.at[d], "gx", to))
    for copy in copies:
        copy.wait_recv()
    own = lines[pl.ds(gx * share, share)]
    for d in range(nx - 1):
        own = own + s2[d]
    waits += copies

    s3[gz] = own
    copies = []
    for d in nearest(nz)[:0:-1]:
        to = lax.rem(gz + d, nz)
        copies.append(send(s3.at[gz], s3.at[gz], out3.at[d], in3.at[d], "gz", to))
    for copy in copies:
        copy.wait_recv()
    waits += copies
    own = s3[0]
    for z in range(1, nz):
        own = own + s3[z]

    s4[gx] = own
    copies = []
    for d in nearest(nx)[:0:-1]:
        to = lax.rem(gx + d, nx)
        copies.append(send(s4.at[gx], s4.at[gx], out4.at[d], in4.at[d], "gx", to))
    for copy in copies:
        copy.wait_recv()
    waits += copies

    result[chunk(gy), :] = jnp.concatenate([s4[x] for x in range(nx)], 0).reshape(part, TILE)
    across = {}
    for f in far_first[:-1]:
        to = lax.rem(chip + f, chips) * 2 + core
        across[f] = send(result.at[chunk(gy)], result.at[chunk(gy)], out5.at[f], in5.at[f], "gy", to)
    copies = []
    for f in far_first[::-1]:
        source = lax.rem(chip + chips - f, chips) * 2 + core
        if f:
            across[f].wait_recv()
        copies.append(send(result.at[chunk(source)], result.at[chunk(source)], out6.at[f], in6.at[f], "gy", partner))
    for copy in copies:
        copy.wait_recv()
    waits += list(across.values()) + copies
    for copy in waits:
        copy.wait_send()


def gram_x_kernel(sizes, field_ref, fibres_ref, gram_ref, field, loaded, outgoing, fibres, partial, result, pair, s1, s2, s3, s4, mine, lines, out0, in0, *sems):
    nx = sizes["gx"]
    gx = lax.axis_index("gx")
    species, planes, rows, width = field_ref.shape
    block = species // nx
    step = planes * width
    order = nearest(nx)[::-1]
    loads = {}
    for d in order:
        part = pl.ds(lax.rem(gx + d, nx) * block, block)
        loads[d] = pltpu.make_async_copy(field_ref.at[part], field.at[part], loaded.at[d])
        loads[d].start()
    greet(sizes)

    def pack(to, put):
        for k in range(block):
            planes_of = [field[to * block + k, z] for z in range(planes)]
            put(k, jnp.concatenate(planes_of, 1))

    own_rows = pl.ds(pl.multiple_of(gx * rows, rows), rows)
    copies = []
    for count, d in enumerate(order[:-1]):
        to = lax.rem(gx + d, nx)

        def put(k, value, d=d):
            outgoing[d - 1, :, k * step : (k + 1) * step] = value

        loads[d].wait()
        pack(to, put)
        if count == 0:
            await_greetings(sizes)
        copies.append(send(outgoing.at[d - 1], fibres.at[own_rows], out0.at[d], in0.at[d], "gx", to))

    def put_own(k, value):
        fibres[own_rows, k * step : (k + 1) * step] = value

    loads[0].wait()
    pack(gx, put_own)
    for copy in copies:
        copy.wait_recv()
    half = fibres.shape[0] // 2
    halves = [fibres[:half, :], fibres[half:, :]]
    fold(partial, lambda i, j: dot(halves[i], halves[j], 1, 1))
    total(partial, result, sizes, pair, s1, s2, s3, s4, mine, lines, sems)
    fibres_ref[...] = fibres[...]
    gram_ref[...] = result[...]
    for copy in copies:
        copy.wait_send()


def gram_y_kernel(sizes, groups, low_ref, fibres_ref, matrix_ref, gram_ref, outgoing, blocks, matrix, partial, result, pair, s1, s2, s3, s4, mine, lines, out0, in0, *sems):
    ny = sizes["gy"]
    gy = lax.axis_index("gy")
    chips = ny // 2
    chip, core = gy // 2, lax.rem(gy, 2)
    part = low_ref.shape[0] // ny
    width = fibres_ref.shape[1] // groups
    greet(sizes)
    outgoing[...] = dot(low_ref[...], fibres_ref[...], 1, 0).astype(bf16)
    await_greetings(sizes)
    copies = {}
    for f in nearest(chips)[::-1]:
        for other in (1, 0):
            if f or other:
                to = lax.rem(chip + f, chips) * 2 + lax.rem(core + other, 2)
                rows = pl.ds(pl.multiple_of(to * part, part), part)
                copies[f, other] = send(
                    outgoing.at[rows], blocks.at[gy], out0.at[f, other], in0.at[f, other], "gy", to
                )
    blocks[gy] = outgoing[pl.ds(pl.multiple_of(gy * part, part), part), :]
    for f in nearest(chips):
        for other in (0, 1):
            if f or other:
                copies[f, other].wait_recv()
        source = lax.rem(chip + chips - f, chips)
        columns = pl.ds(pl.multiple_of(source * TILE, TILE), TILE)
        for g in range(groups):
            pieces = [blocks[source * 2 + h, :, g * width : (g + 1) * width] for h in range(2)]
            matrix[g * part : (g + 1) * part, columns] = jnp.concatenate(pieces, 1)
    half = matrix.shape[1] // 2
    halves = [matrix[:, :half], matrix[:, half:]]
    fold(partial, lambda i, j: dot(halves[i], halves[j], 0, 0))
    total(partial, result, sizes, pair, s1, s2, s3, s4, mine, lines, sems)
    matrix_ref[...] = matrix[...]
    gram_ref[...] = result[...]
    for copy in copies.values():
        copy.wait_send()


def total_scratch(n, sizes):
    nx, ny, nz = sizes["gx"], sizes["gy"], sizes["gz"]
    rows = (n // TILE) * (n // TILE // 2) * CHUNK
    part = rows // ny
    share = part // nx
    chips = ny // 2
    buffers = [
        pltpu.VMEM((rows, TILE), f32),
        pltpu.VMEM((rows, TILE), f32),
        pltpu.VMEM((chips, part, TILE), f32),
        pltpu.VMEM((chips - 1, part, TILE), f32),
        pltpu.VMEM((nx - 1, share, 1, TILE), f32),
        pltpu.VMEM((nz, share, 1, TILE), f32),
        pltpu.VMEM((nx, share, 1, TILE), f32),
        pltpu.VMEM((chips, part, TILE), f32),
        pltpu.VMEM((part, 1, TILE), f32),
    ]
    sems = []
    for size in (chips, chips, nx, nz, nx, chips, chips):
        sems += [pltpu.SemaphoreType.DMA((size,)), pltpu.SemaphoreType.DMA((size,))]
    return rows, buffers, sems


def body(sizes, tensor_field, start_x, start_y):
    species, planes, rows_x, rows_y = tensor_field.shape
    nx, ny, nz = sizes["gx"], sizes["gy"], sizes["gz"]
    all_x, rank_x = start_x.shape
    all_y, rank_y = start_y.shape
    block = species // nx
    groups = block * planes
    width = groups * rows_y
    part = rank_x // ny
    vmem = pl.BlockSpec(memory_space=pltpu.VMEM)

    def communicating(kernel, outs, own, n, size, collective):
        rows, buffers, sems = total_scratch(n, sizes)
        exchange = [pltpu.SemaphoreType.DMA(size), pltpu.SemaphoreType.DMA(size)]
        return pl.pallas_call(
            kernel,
            out_shape=outs + (jax.ShapeDtypeStruct((rows, TILE), f32),),
            in_specs=[pl.BlockSpec(memory_space=pltpu.HBM)] if collective == 0 else [vmem] * 2,
            out_specs=(vmem,) * (len(outs) + 1),
            scratch_shapes=own + buffers + exchange + sems,
            compiler_params=pltpu.CompilerParams(
                collective_id=collective, has_side_effects=True, vmem_limit_bytes=48 << 20
            ),
        )

    fibres, packed_x = communicating(
        functools.partial(gram_x_kernel, sizes),
        (jax.ShapeDtypeStruct((all_x, width), bf16),),
        [
            pltpu.VMEM(tensor_field.shape, bf16),
            pltpu.SemaphoreType.DMA((nx,)),
            pltpu.VMEM((nx - 1, rows_x, width), bf16),
            pltpu.VMEM((all_x, width), bf16),
        ],
        all_x,
        (nx,),
        0,
    )(tensor_field)

    def scratch(n, rank):
        return [
            pltpu.VMEM((n, n), f32),
            pltpu.VMEM((rank, 2 * rank), f32),
            pltpu.VMEM((rank, n), f32),
            pltpu.VMEM((TILE, rank), f32),
        ]

    own_x, low_x = pl.pallas_call(
        functools.partial(basis_x_kernel, 1.0 / (species * planes * nz * all_y)),
        out_shape=(
            jax.ShapeDtypeStruct((all_x // nx, rank_x), f32),
            jax.ShapeDtypeStruct((rank_x, all_x), bf16),
        ),
        in_specs=[vmem] * 2,
        out_specs=(vmem,) * 2,
        scratch_shapes=scratch(all_x, rank_x),
        compiler_params=pltpu.CompilerParams(vmem_limit_bytes=48 << 20),
    )(packed_x, start_x)

    matrix, packed_y = communicating(
        functools.partial(gram_y_kernel, sizes, groups),
        (jax.ShapeDtypeStruct((groups * part, all_y), bf16),),
        [
            pltpu.VMEM((rank_x, width), bf16),
            pltpu.VMEM((ny, part, width), bf16),
            pltpu.VMEM((groups * part, all_y), bf16),
        ],
        all_y,
        (ny // 2, 2),
        1,
    )(low_x, fibres)

    own_y, core = pl.pallas_call(
        functools.partial(basis_y_kernel, 1.0 / (species * planes * nz * rank_x)),
        out_shape=(
            jax.ShapeDtypeStruct((all_y // ny, rank_y), f32),
            jax.ShapeDtypeStruct((groups * part, rank_y), bf16),
        ),
        in_specs=[vmem] * 3,
        out_specs=(vmem,) * 2,
        scratch_shapes=scratch(all_y, rank_y),
        compiler_params=pltpu.CompilerParams(vmem_limit_bytes=48 << 20),
    )(packed_y, start_y, matrix)
    return own_x, own_y, core.reshape(block, planes, part, rank_y)


def solution(mesh):
    sizes = {axis: mesh.shape[axis] for axis in ("gx", "gy", "gz")}
    in_specs = (P(None, "gz", "gx", "gy"), P(), P())
    out_specs = (P("gx", None), P("gy", None), P("gx", "gz", "gy", None))
    return jax.shard_map(
        functools.partial(body, sizes), mesh=mesh, in_specs=in_specs, out_specs=out_specs, check_vma=False
    )
```

```python
import functools

import jax
import jax.numpy as jnp
from jax import lax
from jax.experimental import pallas as pl
from jax.experimental.pallas import tpu as pltpu
from jax.sharding import PartitionSpec as P

ITERS = 3
PANEL = 32
SPREAD = 16
TILE = 128
CHUNK = TILE + 8
MESH = pl.DeviceIdType.MESH
f32 = jnp.float32
bf16 = jnp.bfloat16


def split3(value):
    high = value.astype(bf16)
    rest = value - high.astype(f32)
    middle = rest.astype(bf16)
    low = (rest - middle.astype(f32)).astype(bf16)
    return high, middle, low


def factor(work):
    n = work.shape[0]
    sub = lax.broadcasted_iota(jnp.int32, (8, TILE), 0)
    for top in range(0, n, PANEL):
        below = top + PANEL
        first = (top // TILE) * TILE
        last = -(-below // TILE) * TILE
        lanes = list(range(first, n, TILE)) + list(range(n, n + last, TILE))

        def wide(value):
            return jnp.concatenate([value] * len(lanes), 1)

        rest = jnp.concatenate([work[top:below, at : at + TILE] for at in lanes], 1)
        finished = []
        for start in range(0, PANEL, SPREAD):
            offset = top + start - first
            rows = PANEL - start
            spread = jnp.stack(
                [jnp.broadcast_to(rest[:, offset + k : offset + k + 1], (rows, TILE)) for k in range(SPREAD)]
            )
            for j in range(SPREAD):
                i = j % 8
                if i == 0:
                    scales = jnp.ones((8, TILE), f32)
                column = spread[0]
                scale = lax.rsqrt(column[i : i + 1, :])
                scales = jnp.where(sub == i, scale, scales)
                times = column * scale
                times = [jnp.where(sub > i, times[:8], 0.0)] + ([times[8:]] if times.shape[0] > 8 else [])
                times = jnp.concatenate(times, 0)
                rest = rest - wide(times) * (rest[i : i + 1, :] * wide(scale))
                if j + 1 < SPREAD:
                    spread = spread[1:] - times[None] * (spread[1:, i : i + 1, :] * scale[None])
                if i == 7:
                    finished.append(rest[:8] * wide(scales))
                    rest = rest[8:]
                    if j + 1 < SPREAD:
                        spread = spread[:, 8:]
        done = jnp.concatenate(finished, 0)
        for a, at in enumerate(lanes):
            if at >= n:
                work[top:below, at : at + TILE] = done[:, TILE * a : TILE * (a + 1)]
        if below < n:
            high, middle, low = split3(done)
            right = jnp.concatenate([high, middle, low, high, middle, high], 0)
            left = jnp.concatenate([high, high, high, middle, middle, low], 0)[:, : n - first]
            update = lax.dot_general(left, right, (((0,), (0,)), ((), ())), preferred_element_type=f32)
            update = update[below - first :, :]
            for a, at in enumerate(lanes):
                work[below:, at : at + TILE] -= update[:, TILE * a : TILE * (a + 1)]


def masks(size):
    row = lax.broadcasted_iota(jnp.int32, (size, size), 0)
    column = lax.broadcasted_iota(jnp.int32, (size, size), 1)
    return row, column


def fold(partial, block):
    lower, first, second = block(1, 0), block(0, 0), block(1, 1)
    half = first.shape[0]
    row, column = masks(half)
    mixed = jnp.where(row > column, second, first)
    diagonal = jnp.sum(jnp.where(row == column, second, 0.0), axis=0, keepdims=True)
    sub = lax.broadcasted_iota(jnp.int32, (8, TILE), 0)
    at = 0
    for whole in (lower, mixed):
        for c in range(0, half, TILE):
            for r in range(0, half, TILE):
                partial[at : at + TILE, :] = whole[r : r + TILE, c : c + TILE]
                chunk = at // CHUNK
                if chunk * TILE < half:
                    piece = diagonal[:, chunk * TILE : (chunk + 1) * TILE]
                    extra = jnp.where(sub == 0, jnp.broadcast_to(piece, (8, TILE)), 0.0)
                else:
                    extra = jnp.zeros((8, TILE), f32)
                partial[at + TILE : at + CHUNK, :] = extra
                at += CHUNK


def unfold(packed_ref, gram_ref, scale):
    half = gram_ref.shape[0] // 2
    row, column = masks(half)
    side = half // TILE

    def whole(first):
        columns = []
        for c in range(side):
            starts = [(first + c * side + r) * CHUNK for r in range(side)]
            columns.append(jnp.concatenate([packed_ref[at : at + TILE, :] for at in starts], 0))
        return jnp.concatenate(columns, 1) * scale

    lower, mixed = whole(0), whole(side * side)
    ends = [packed_ref[k * CHUNK + TILE : k * CHUNK + TILE + 1, :] for k in range(side)]
    diagonal = jnp.broadcast_to(jnp.concatenate(ends, 1) * scale, (half, half))
    turned = mixed.T
    gram_ref[:half, :half] = jnp.where(row <= column, mixed, turned)
    gram_ref[:half, half:] = lower.T
    gram_ref[half:, :half] = lower
    gram_ref[half:, half:] = jnp.where(row > column, mixed, jnp.where(row == column, diagonal, turned))


def dot(left, right, left_axis, right_axis):
    return lax.dot_general(left, right, (((left_axis,), (right_axis,)), ((), ())), preferred_element_type=f32)


def dot3(left, right, left_axis, right_axis):
    (a, b, _), (c, d, _) = left, right
    return (dot(b, c, left_axis, right_axis) + dot(a, d, left_axis, right_axis)) + dot(a, c, left_axis, right_axis)


def inner(value):
    high, middle, low = value
    cross = dot(high, low, 1, 1) + dot(high, middle, 1, 1)
    return (dot(middle, middle, 1, 1) + (cross + cross.T)) + dot(high, high, 1, 1)


def subspace(gram_ref, start, work):
    rank = work.shape[0]
    row, column = masks(rank)
    gram = split3(gram_ref[...])
    for sweep in range(ITERS):
        if sweep == 0:
            product = split3(dot3(split3(start), gram, 0, 0))
        else:
            product = split3(dot3(split3(current), gram, 1, 0))
        work[:, :rank] = inner(product)
        work[:, rank:] = jnp.where(row == column, 1.0, 0.0)
        factor(work)
        current = dot3(split3(work[:, rank:]), product, 1, 0)
    return current


def subspace_loop(gram_ref, parts, basis, work):
    rank = work.shape[0]
    row, column = masks(rank)
    parts[0], parts[1], _ = split3(gram_ref[...])

    @pl.loop(0, ITERS)
    def _(sweep):
        product = split3(dot3(split3(basis[...]), (parts[0], parts[1], None), 1, 0))
        work[:, :rank] = inner(product)
        work[:, rank:] = jnp.where(row == column, 1.0, 0.0)
        factor(work)
        basis[...] = dot3(split3(work[:, rank:]), product, 1, 0)


def own_rows(basis, axis, own_ref, block):
    rows = own_ref.shape[0]
    shares = TILE // rows
    me = lax.axis_index(axis)
    block[...] = basis[:, pl.ds(pl.multiple_of(me // shares * TILE, TILE), TILE)].T
    own_ref[...] = block[pl.ds(pl.multiple_of(lax.rem(me, shares) * rows, rows), rows), :]


def basis_y_kernel(scale, packed_ref, start_ref, field_ref, own_x_ref, own_ref, core_ref, kept_ref, gram, work, basis, block):
    kept_ref[...] = own_x_ref[...]
    unfold(packed_ref, gram, scale)
    basis[...] = subspace(gram, start_ref[...], work)
    core_ref[...] = dot(field_ref[...], basis[...].astype(bf16), 1, 1).astype(bf16)
    own_rows(basis, "gy", own_ref, block)


def send(source, target, send_sem, recv_sem, axis, device):
    copy = pltpu.make_async_remote_copy(
        src_ref=source,
        dst_ref=target,
        send_sem=send_sem,
        recv_sem=recv_sem,
        device_id={axis: device},
        device_id_type=MESH,
    )
    copy.start()
    return copy


def greet(sizes):
    barrier = pltpu.get_barrier_semaphore()
    for axis, size in sizes.items():
        me = lax.axis_index(axis)
        for d in range(1, size):
            pl.semaphore_signal(
                barrier, inc=1, device_id={axis: lax.rem(me + d, size)}, device_id_type=MESH
            )


def await_greetings(sizes):
    pl.semaphore_wait(pltpu.get_barrier_semaphore(), sum(size - 1 for size in sizes.values()))


def nearest(size):
    return sorted(range(size), key=lambda d: min(d, size - d))


def total(partial, result, sizes, pair, s1, s2, s3, s4, mine, lines, sems):
    nx, ny, nz = sizes["gx"], sizes["gy"], sizes["gz"]
    gx, gy, gz = lax.axis_index("gx"), lax.axis_index("gy"), lax.axis_index("gz")
    chips = ny // 2
    core = lax.rem(gy, 2)
    chip = gy // 2
    partner = gy + 1 - 2 * core
    part = partial.shape[0] // ny
    share = part // nx
    out0, in0, out1, in1, out2, in2, out3, in3, out4, in4, out5, in5, out6, in6 = sems
    waits = []

    def chunk(index):
        return pl.ds(pl.multiple_of(index * part, 8), part)

    far_first = nearest(chips)[::-1]
    given = {}
    for f in far_first:
        to = lax.rem(chip + f, chips) * 2 + 1 - core
        given[f] = send(partial.at[chunk(to)], pair.at[f], out0.at[f], in0.at[f], "gy", partner)
    scattered = []
    for f in far_first:
        to = lax.rem(chip + f, chips) * 2 + core
        given[f].wait_recv()
        mine[f] = partial[chunk(to), :] + pair[f]
        if f:
            scattered.append(send(mine.at[f], s1.at[f - 1], out1.at[f], in1.at[f], "gy", to))
    for copy in scattered:
        copy.wait_recv()
    own = mine[0]
    for f in range(chips - 1):
        own = own + s1[f]
    lines[...] = own.reshape(lines.shape)
    waits += list(given.values()) + scattered

    copies = []
    for d in nearest(nx)[:0:-1]:
        to = lax.rem(gx + d, nx)
        copies.append(send(lines.at[pl.ds(to * share, share)], s2.at[d - 1], out2.at[d], in2.at[d], "gx", to))
    for copy in copies:
        copy.wait_recv()
    own = lines[pl.ds(gx * share, share)]
    for d in range(nx - 1):
        own = own + s2[d]
    waits += copies

    s3[gz] = own
    copies = []
    for d in nearest(nz)[:0:-1]:
        to = lax.rem(gz + d, nz)
        copies.append(send(s3.at[gz], s3.at[gz], out3.at[d], in3.at[d], "gz", to))
    for copy in copies:
        copy.wait_recv()
    waits += copies
    own = s3[0]
    for z in range(1, nz):
        own = own + s3[z]

    s4[gx] = own
    copies = []
    for d in nearest(nx)[:0:-1]:
        to = lax.rem(gx + d, nx)
        copies.append(send(s4.at[gx], s4.at[gx], out4.at[d], in4.at[d], "gx", to))
    for copy in copies:
        copy.wait_recv()
    waits += copies

    result[chunk(gy), :] = jnp.concatenate([s4[x] for x in range(nx)], 0).reshape(part, TILE)
    across = {}
    for f in far_first[:-1]:
        to = lax.rem(chip + f, chips) * 2 + core
        across[f] = send(result.at[chunk(gy)], result.at[chunk(gy)], out5.at[f], in5.at[f], "gy", to)
    copies = []
    for f in far_first[::-1]:
        source = lax.rem(chip + chips - f, chips) * 2 + core
        if f:
            across[f].wait_recv()
        copies.append(send(result.at[chunk(source)], result.at[chunk(source)], out6.at[f], in6.at[f], "gy", partner))
    for copy in copies:
        copy.wait_recv()
    waits += list(across.values()) + copies
    for copy in waits:
        copy.wait_send()


def gram_x(sizes, field_ref, start_ref, basis, field, loaded, outgoing, fibres, exchange, buffers, sems):
    out0, in0 = exchange
    partial, result = buffers[:2]
    nx = sizes["gx"]
    gx = lax.axis_index("gx")
    species, planes, rows, width = field_ref.shape
    block = species // nx
    step = planes * width
    order = nearest(nx)[::-1]
    loads = {}
    for d in order:
        part = pl.ds(lax.rem(gx + d, nx) * block, block)
        loads[d] = pltpu.make_async_copy(field_ref.at[part], field.at[part], loaded.at[d])
        loads[d].start()
    greet(sizes)

    def pack(to, put):
        for k in range(block):
            planes_of = [field[to * block + k, z] for z in range(planes)]
            put(k, jnp.concatenate(planes_of, 1))

    own_rows = pl.ds(pl.multiple_of(gx * rows, rows), rows)
    copies = []
    for count, d in enumerate(order[:-1]):
        to = lax.rem(gx + d, nx)

        def put(k, value, d=d):
            outgoing[d - 1, :, k * step : (k + 1) * step] = value

        loads[d].wait()
        pack(to, put)
        if count == 0:
            await_greetings(sizes)
        copies.append(send(outgoing.at[d - 1], fibres.at[own_rows], out0.at[d], in0.at[d], "gx", to))

    def put_own(k, value):
        fibres[own_rows, k * step : (k + 1) * step] = value

    loads[0].wait()
    pack(gx, put_own)
    basis[...] = start_ref[...].T
    for copy in copies:
        copy.wait_recv()
    half = fibres.shape[0] // 2
    halves = [fibres[:half, :], fibres[half:, :]]
    fold(partial, lambda i, j: dot(halves[i], halves[j], 1, 1))
    total(partial, result, sizes, *buffers[2:], sems)
    for copy in copies:
        copy.wait_send()


def gram_y(sizes, groups, low, fibres, outgoing, blocks, matrix, exchange, buffers, sems):
    out0, in0 = exchange
    partial, result = buffers[:2]
    ny = sizes["gy"]
    gy = lax.axis_index("gy")
    chips = ny // 2
    chip, core = gy // 2, lax.rem(gy, 2)
    part = low.shape[0] // ny
    width = fibres.shape[1] // groups
    outgoing[...] = dot(low, fibres[...], 1, 0).astype(bf16)
    copies = {}
    for f in nearest(chips)[::-1]:
        for other in (1, 0):
            if f or other:
                to = lax.rem(chip + f, chips) * 2 + lax.rem(core + other, 2)
                rows = pl.ds(pl.multiple_of(to * part, part), part)
                copies[f, other] = send(
                    outgoing.at[rows], blocks.at[gy], out0.at[f, other], in0.at[f, other], "gy", to
                )
    blocks[gy] = outgoing[pl.ds(pl.multiple_of(gy * part, part), part), :]
    for f in nearest(chips):
        for other in (0, 1):
            if f or other:
                copies[f, other].wait_recv()
        source = lax.rem(chip + chips - f, chips)
        columns = pl.ds(pl.multiple_of(source * TILE, TILE), TILE)
        for g in range(groups):
            pieces = [blocks[source * 2 + h, :, g * width : (g + 1) * width] for h in range(2)]
            matrix[g * part : (g + 1) * part, columns] = jnp.concatenate(pieces, 1)
    half = matrix.shape[1] // 2
    halves = [matrix[:, :half], matrix[:, half:]]
    fold(partial, lambda i, j: dot(halves[i], halves[j], 0, 0))
    total(partial, result, sizes, *buffers[2:], sems)
    for copy in copies.values():
        copy.wait_send()


def first_kernel(sizes, groups, scale, counts, field_ref, start_ref, own_ref, matrix_ref, gram_ref, *scratch):
    scratch = list(scratch)

    def take(count):
        taken = scratch[:count]
        del scratch[:count]
        return taken

    field, loaded, outgoing_x, fibres = take(4)
    gram, parts, work, basis, block = take(5)
    outgoing_y, blocks, matrix = take(3)
    buffers_x, sems_x, buffers_y, sems_y = [take(count) for count in counts]
    gram_x(sizes, field_ref, start_ref, basis, field, loaded, outgoing_x, fibres, sems_x[:2], buffers_x, sems_x[2:])
    unfold(buffers_x[1], gram, scale)
    subspace_loop(gram, parts, basis, work)
    gram_y(
        sizes, groups, basis[...].astype(bf16), fibres, outgoing_y, blocks, matrix, sems_y[:2], buffers_y, sems_y[2:]
    )
    own_rows(basis, "gx", own_ref, block)
    matrix_ref[...] = matrix[...]
    gram_ref[...] = buffers_y[1][...]


def total_scratch(n, sizes):
    nx, ny, nz = sizes["gx"], sizes["gy"], sizes["gz"]
    rows = (n // TILE) * (n // TILE // 2) * CHUNK
    part = rows // ny
    share = part // nx
    chips = ny // 2
    buffers = [
        pltpu.VMEM((rows, TILE), f32),
        pltpu.VMEM((rows, TILE), f32),
        pltpu.VMEM((chips, part, TILE), f32),
        pltpu.VMEM((chips - 1, part, TILE), f32),
        pltpu.VMEM((nx - 1, share, 1, TILE), f32),
        pltpu.VMEM((nz, share, 1, TILE), f32),
        pltpu.VMEM((nx, share, 1, TILE), f32),
        pltpu.VMEM((chips, part, TILE), f32),
        pltpu.VMEM((part, 1, TILE), f32),
    ]
    sems = []
    for size in (chips, chips, nx, nz, nx, chips, chips):
        sems += [pltpu.SemaphoreType.DMA((size,)), pltpu.SemaphoreType.DMA((size,))]
    return rows, buffers, sems


def body(sizes, tensor_field, start_x, start_y):
    species, planes, rows_x, rows_y = tensor_field.shape
    nx, ny, nz = sizes["gx"], sizes["gy"], sizes["gz"]
    all_x, rank_x = start_x.shape
    all_y, rank_y = start_y.shape
    block = species // nx
    groups = block * planes
    width = groups * rows_y
    part = rank_x // ny
    vmem = pl.BlockSpec(memory_space=pltpu.VMEM)

    def scratch(n, rank):
        return [
            pltpu.VMEM((n, n), f32),
            pltpu.VMEM((rank, 2 * rank), f32),
            pltpu.VMEM((rank, n), f32),
            pltpu.VMEM((TILE, rank), f32),
        ]

    gram, work, basis, own = scratch(all_x, rank_x)
    single = [
        pltpu.VMEM(tensor_field.shape, bf16),
        pltpu.SemaphoreType.DMA((nx,)),
        pltpu.VMEM((nx - 1, rows_x, width), bf16),
        pltpu.VMEM((all_x, width), bf16),
        gram,
        pltpu.VMEM((2, all_x, all_x), bf16),
        work,
        basis,
        own,
        pltpu.VMEM((rank_x, width), bf16),
        pltpu.VMEM((ny, part, width), bf16),
        pltpu.VMEM((groups * part, all_y), bf16),
    ]
    rows, buffers_x, sems_x = total_scratch(all_x, sizes)
    rows, buffers_y, sems_y = total_scratch(all_y, sizes)
    sems_x = [pltpu.SemaphoreType.DMA((nx,))] * 2 + sems_x
    sems_y = [pltpu.SemaphoreType.DMA((ny // 2, 2))] * 2 + sems_y
    counts = [len(refs) for refs in (buffers_x, sems_x, buffers_y, sems_y)]
    own_x, matrix, packed_y = pl.pallas_call(
        functools.partial(
            first_kernel, sizes, groups, 1.0 / (species * planes * nz * all_y), counts
        ),
        out_shape=(
            jax.ShapeDtypeStruct((all_x // nx, rank_x), f32),
            jax.ShapeDtypeStruct((groups * part, all_y), bf16),
            jax.ShapeDtypeStruct((rows, TILE), f32),
        ),
        in_specs=[pl.BlockSpec(memory_space=pltpu.HBM), vmem],
        out_specs=(vmem,) * 3,
        scratch_shapes=single + buffers_x + sems_x + buffers_y + sems_y,
        compiler_params=pltpu.CompilerParams(
            collective_id=0, has_side_effects=True, vmem_limit_bytes=48 << 20
        ),
    )(tensor_field, start_x)

    own_y, core, own_x = pl.pallas_call(
        functools.partial(basis_y_kernel, 1.0 / (species * planes * nz * rank_x)),
        out_shape=(
            jax.ShapeDtypeStruct((all_y // ny, rank_y), f32),
            jax.ShapeDtypeStruct((groups * part, rank_y), bf16),
            jax.ShapeDtypeStruct((all_x // nx, rank_x), f32),
        ),
        in_specs=[vmem] * 4,
        out_specs=(vmem,) * 3,
        scratch_shapes=scratch(all_y, rank_y),
        compiler_params=pltpu.CompilerParams(vmem_limit_bytes=48 << 20),
    )(packed_y, start_y, matrix, own_x)
    return own_x, own_y, core.reshape(block, planes, part, rank_y)


def solution(mesh):
    sizes = {axis: mesh.shape[axis] for axis in ("gx", "gy", "gz")}
    in_specs = (P(None, "gz", "gx", "gy"), P(), P())
    out_specs = (P("gx", None), P("gy", None), P("gx", "gz", "gy", None))
    return jax.shard_map(
        functools.partial(body, sizes), mesh=mesh, in_specs=in_specs, out_specs=out_specs, check_vma=False
    )
```
